1024 devices in a mesh: dp: 8 (over x, core), shard: 128 (over z, y).
Axes of the slice: x: 4, y: 4, z: 32, core: 2. Of those that a mesh axis runs over, the one named last changes fastest.
Arguments:
- gradients: float32 [8, 3, 448, 32768], P('dp', None, None, 'shard'), may hold values from -6 to 6
- momentum: float32 [3, 448, 32768], P(None, 'dp', 'shard'), may hold values from -6 to 6
Outputs:
- momentum_out: float32 [3, 448, 32768], P(None, 'dp', 'shard')
- update: bfloat16 [3, 448, 32768], P(None, 'dp', 'shard')
The draws below stay inside these ranges and needn't reach their ends.
All inputs are finite; a program needn't handle non-finite values.
Results may differ from the reference program's by a relative error of at most 0.018.
The reference program's roundings to bfloat16 on the way count: a program that leaves them out, or rounds other values in their place, can miss the bound.
Values may be sent and summed in bfloat16 or wider, within the bound.
No kernel may reach another device: no remote copies, remote signals or barrier semaphores. Data moves between devices by JAX's collectives and lax.ppermute only.
A program may use at most 128 MiB of HBM per device.

```python
import jax
import jax.numpy as jnp
from jax import lax

R = 7168
C = 2048
ITERS = 5
BR = 16
E = 3
RB = 448
N_DP = 8


def raised(entries, rng, source, target, parts, factor):
    owner, partner = [(jnp.arange(entries.shape[axis_at]) // (entries.shape[axis_at] // parts)).reshape([-1 if axis == axis_at else 1 for axis in range(entries.ndim)]) for axis_at in (source, target)]
    chosen = jax.random.permutation(rng, parts)[partner]
    strong = (owner == chosen) | (owner == (partner + parts // 2) % parts)
    return jnp.where(strong, factor * entries, entries)


def shard_levels(stream_key, dims, split, low, top_value):
    factor_of = 1.0
    for axis_at, blocks in split:
        draws = jax.random.uniform(jax.random.fold_in(jax.random.fold_in(stream_key, 6), axis_at), (blocks,), jnp.float32, low / len(split), top_value / len(split))
        factor_of = factor_of * jnp.repeat(jnp.exp(draws), dims[axis_at] // blocks).reshape((-1,) + (1,) * (len(dims) - 1 - axis_at))
    return factor_of


def normal_values(own_key, dims, deviation, reach, shards=(), held_as=jnp.bfloat16):
    entries = jax.random.normal(own_key, dims, jnp.float32) * deviation
    if len(shards) > 0:
        entries = shard_levels(own_key, dims, shards, -0.22, 0.18) * entries
    return jnp.clip(entries, min=-reach, max=reach).astype(held_as)


def heavy_noise(stream_key, shape, spread, most, split, heavy, kind=jnp.bfloat16):
    drawn = spread * jax.random.normal(stream_key, shape, jnp.float32)
    if split:
        drawn = drawn * shard_levels(stream_key, shape, split, -0.22, 0.18)
    return jnp.clip(raised(drawn, jax.random.fold_in(stream_key, 3), *heavy), -most, most).astype(kind)


def setup_inputs(seed: int = 0) -> dict:
    streams_of = jax.random.split(jax.random.key(seed), 3)
    gradients = heavy_noise(streams_of[0], (N_DP, E, RB, BR * C), 1.0, 6.0, ((0, 8), (3, 128)), (0, 2, 8, 2.0), jnp.float32)
    momentum = normal_values(streams_of[1], (E, RB, BR * C), 1.0, 6.0, ((1, 8), (2, 128)), jnp.float32)
    return {"gradients": gradients, "momentum": momentum}


COEF_A = 3.4445
COEF_B = -4.775
COEF_C = 2.0315
DECAY = 0.95
EPSILON = 1e-07
ROW_SCALE = 0.2

def newton_schulz(flat_blocks):
    blocks = flat_blocks.reshape(flat_blocks.shape[0], BR, C)
    squares = lax.optimization_barrier(jnp.sum(jnp.square(blocks.astype(jnp.float32)), axis=(1, 2)))
    current = (blocks.astype(jnp.float32) / (jnp.sqrt(squares) + EPSILON)[:, None, None]).astype(jnp.bfloat16)
    for sweep_index in range(ITERS):
        wide_current = current.astype(jnp.float32)
        gram = jnp.einsum('kri,ksi->krs', wide_current, wide_current, precision=lax.Precision.HIGHEST).astype(jnp.bfloat16)
        wide_gram = gram.astype(jnp.float32)
        squared = jnp.einsum('krs,kst->krt', wide_gram, wide_gram, precision=lax.Precision.HIGHEST)
        polynomial = (COEF_B * wide_gram + COEF_C * squared).astype(jnp.bfloat16)
        product = jnp.einsum('krs,ksi->kri', polynomial.astype(jnp.float32), wide_current, precision=lax.Precision.HIGHEST)
        current = (COEF_A * wide_current + product).astype(jnp.bfloat16)
    factor = ROW_SCALE * jnp.sqrt(jnp.float32(R))
    result = (current.astype(jnp.float32) * factor).astype(jnp.bfloat16)
    return result.reshape(flat_blocks.shape)

def reference(gradients, momentum):
    summed = lax.optimization_barrier(jnp.sum(gradients, axis=0))
    momentum_next = DECAY * momentum + summed
    nesterov = (summed + DECAY * momentum_next).astype(jnp.bfloat16)
    update = lax.map(newton_schulz, nesterov)
    return (momentum_next, update)
```

```python
import jax
import jax.numpy as jnp
from jax import lax
from jax.experimental import pallas as pl
from jax.experimental.pallas import tpu as pltpu
from jax.sharding import PartitionSpec as P

R = 7168
C = 2048
ITERS = 5
BR = 16

COEF_A = 3.4445
COEF_B = -4.775
COEF_C = 2.0315
DECAY = 0.95
EPSILON = 1e-07
ROW_SCALE = 0.2

F32 = jnp.float32
BF16 = jnp.bfloat16
GROUP = 8
HALVES = 2
SLOTS = GROUP * HALVES


def dot(a, b):
    return jnp.dot(a, b, preferred_element_type=F32)


def split(a):
    high = a.astype(BF16)
    rest = a - high.astype(F32)
    middle = rest.astype(BF16)
    low = (rest - middle.astype(F32)).astype(BF16)
    return high, middle, low


def same_block(size):
    rows = lax.broadcasted_iota(jnp.int32, (size, size), 0)
    columns = lax.broadcasted_iota(jnp.int32, (size, size), 1)
    return rows % GROUP == columns % GROUP


def half_of(rows_ref, half):
    wide = rows_ref[...].astype(F32)
    width = wide.shape[-1]
    return wide.reshape(BR, HALVES, GROUP, width)[:, half].reshape(BR * GROUP, width)


def gram_kernel(rows_ref, gram_ref):
    size = BR * GROUP
    mask = same_block(size)
    for half in range(HALVES):
        rows = half_of(rows_ref, half).astype(BF16)
        full = lax.dot_general(rows, rows, (((1,), (1,)), ((), ())), preferred_element_type=F32)
        full = jnp.where(mask, full, 0.0)
        part = jnp.sum(full.reshape(BR, GROUP, size), axis=1)
        for peer in range(gram_ref.shape[0]):
            gram_ref[peer, half] = part


def sweep_kernel(grams_ref, rows_ref, out_ref):
    size = BR * GROUP
    mask = same_block(size)
    same = lax.broadcasted_iota(jnp.int32, (size, size), 0) == lax.broadcasted_iota(jnp.int32, (size, size), 1)
    results = []
    for half in range(HALVES):
        gram = jnp.sum(grams_ref[:, half], axis=0)
        width = gram.shape[-1]
        full = jnp.broadcast_to(gram[:, None, :], (BR, GROUP, width)).reshape(size, size)
        full = jnp.where(mask, full, 0.0)
        diagonal = jnp.where(same, full, 0.0)
        by_column = jnp.sum(diagonal, axis=0, keepdims=True)
        squares = jnp.sum(jnp.where(mask, by_column, 0.0), axis=1, keepdims=True)
        norm = jnp.sqrt(squares) + EPSILON
        inverse = 1.0 / norm
        wide_gram = full * (inverse * inverse)
        current = (half_of(rows_ref, half) / norm).astype(BF16)
        for sweep_index in range(ITERS):
            high, middle, low = split(wide_gram)
            squared = dot(high, high)
            polynomial = (COEF_B * high.astype(F32) + COEF_C * squared).astype(BF16)
            current = (COEF_A * current.astype(F32) + dot(polynomial, current)).astype(BF16)
            if sweep_index + 1 < ITERS:
                left = COEF_A * wide_gram + (dot(polynomial, low) + dot(polynomial, middle) + dot(polynomial, high))
                high, middle, low = split(left)
                wide_gram = COEF_A * left + (dot(low, polynomial) + dot(middle, polynomial) + dot(high, polynomial))
        factor = ROW_SCALE * (float(R) ** 0.5)
        results.append((current.astype(F32) * factor).reshape(BR, 1, GROUP, -1))
    out_ref[...] = jnp.concatenate(results, axis=1).reshape(out_ref.shape).astype(BF16)


def vmem_call(kernel, shape, dtype, count, flops):
    return pl.pallas_call(
        kernel,
        out_shape=jax.ShapeDtypeStruct(shape, dtype),
        in_specs=[pl.BlockSpec(memory_space=pltpu.VMEM)] * count,
        out_specs=pl.BlockSpec(memory_space=pltpu.VMEM),
        cost_estimate=pl.CostEstimate(flops=flops, bytes_accessed=0, transcendentals=0),
    )


def owner_groups():
    chunks = C // 256
    return [[row * chunks + chunk for row in range(BR)] for chunk in range(chunks)]


def chunk_groups():
    chunks = C // 256
    return [[row * chunks + chunk for chunk in range(chunks)] for row in range(BR)]


def gather_sum(gradients):
    groups = lax.axis_size("dp")
    mats, blocks, width = gradients.shape
    parts = gradients.astype(BF16).reshape(mats, groups, blocks // groups, width).swapaxes(0, 1)
    arrived = lax.all_to_all(parts, "dp", 0, 0, tiled=True)
    return jnp.sum(arrived.astype(F32), axis=0)


def shards(gradients, momentum):
    mats, local, width = momentum.shape
    count = mats * local
    summed = gather_sum(gradients[0])
    momentum_next = DECAY * momentum + summed
    nesterov = (summed + DECAY * momentum_next).astype(BF16).reshape(count, width)
    padded = jnp.pad(nesterov, ((0, HALVES * BR * GROUP - count), (0, 0)))
    outgoing = padded.reshape(HALVES, BR, GROUP, width).swapaxes(0, 1).reshape(BR, SLOTS, width)
    rows = lax.all_to_all(outgoing, "shard", 0, 0, tiled=True, axis_index_groups=owner_groups())
    rows = rows.reshape(BR * SLOTS, width)
    chunks = C // width
    parts = vmem_call(gram_kernel, (chunks, HALVES, BR, BR * GROUP), F32, 1, 0)(rows)
    grams = lax.all_to_all(parts, "shard", 0, 0, tiled=True, axis_index_groups=chunk_groups())
    finished = vmem_call(sweep_kernel, rows.shape, BF16, 2, 0)(grams, rows)
    returned = lax.all_to_all(
        finished.reshape(BR, SLOTS, width), "shard", 0, 0, tiled=True, axis_index_groups=owner_groups()
    )
    flat = returned.reshape(BR, HALVES, GROUP, width).swapaxes(0, 1).reshape(HALVES * BR * GROUP, width)
    return momentum_next, flat[:count].reshape(momentum.shape)


def solution(mesh):
    placed = (P("dp", None, None, "shard"), P(None, "dp", "shard"))
    return jax.shard_map(
        shards,
        mesh=mesh,
        in_specs=placed,
        out_specs=(P(None, "dp", "shard"), P(None, "dp", "shard")),
        check_vma=False,
    )
```

```python
import jax
import jax.numpy as jnp
from jax import lax
from jax.experimental import pallas as pl
from jax.experimental.pallas import tpu as pltpu
from jax.sharding import PartitionSpec as P

R = 7168
C = 2048
ITERS = 5
BR = 16

COEF_A = 3.4445
COEF_B = -4.775
COEF_C = 2.0315
DECAY = 0.95
EPSILON = 1e-07
ROW_SCALE = 0.2

F32 = jnp.float32
BF16 = jnp.bfloat16
LANES = 128
GROUP = 8
HALF = GROUP // 2
SIZE = BR * GROUP
TILES = 3


def dot(a, b):
    return jnp.dot(a, b, preferred_element_type=F32)


def split(a):
    high = a.astype(BF16)
    return high, (a - high.astype(F32)).astype(BF16)


def pack(rows):
    owners = BR
    count, width = rows.shape
    first = owners * GROUP
    halves = rows[:first].reshape(owners, GROUP, 2, LANES).swapaxes(1, 2)
    others = rows[first:].reshape((count - first) // HALF, HALF, 2, LANES).swapaxes(1, 2)
    others = others.reshape(-1, 1, GROUP, LANES)
    others = jnp.pad(others, ((0, owners - others.shape[0]), (0, 0), (0, 0), (0, 0)))
    return jnp.concatenate([halves, others], axis=1)


def unpack(tiles, count):
    owners = BR
    first = owners * GROUP
    halves = tiles[:, :2].swapaxes(1, 2).reshape(first, 2 * LANES)
    others = tiles[: (count - first) // HALF, 2].reshape(-1, 2, HALF, LANES).swapaxes(1, 2)
    return jnp.concatenate([halves, others.reshape(count - first, 2 * LANES)], axis=0)


def row_groups(rows_ref):
    wide = rows_ref[...].astype(F32)
    tiles = [wide[:, tile].reshape(SIZE, LANES) for tile in range(TILES)]
    return [jnp.concatenate(tiles[:2], axis=1), tiles[2]]


def same_slot():
    rows = lax.broadcasted_iota(jnp.int32, (SIZE, SIZE), 0)
    columns = lax.broadcasted_iota(jnp.int32, (SIZE, SIZE), 1)
    return rows % GROUP == columns % GROUP


def gram_kernel(rows_ref, gram_ref):
    mask = same_slot()
    parts = []
    for rows in row_groups(rows_ref):
        rows = rows.astype(BF16)
        full = lax.dot_general(rows, rows, (((1,), (1,)), ((), ())), preferred_element_type=F32)
        parts.append(jnp.sum(jnp.where(mask, full, 0.0).reshape(BR, GROUP, SIZE), axis=1))
    halves = parts[1]
    lane = lax.broadcasted_iota(jnp.int32, halves.shape, 1)
    other = jnp.where(lane % GROUP < HALF, pltpu.roll(halves, SIZE - HALF, 1), pltpu.roll(halves, HALF, 1))
    parts[1] = halves + other
    for peer in range(gram_ref.shape[0]):
        for group, part in enumerate(parts):
            gram_ref[peer, group] = part


def sweep_kernel(grams_ref, rows_ref, out_ref):
    mask = same_slot()
    same = lax.broadcasted_iota(jnp.int32, (SIZE, SIZE), 0) == lax.broadcasted_iota(jnp.int32, (SIZE, SIZE), 1)
    grams = []
    currents = []
    for group, rows in enumerate(row_groups(rows_ref)):
        gram = jnp.sum(grams_ref[:, group], axis=0)
        full = jnp.broadcast_to(gram[:, None, :], (BR, GROUP, SIZE)).reshape(SIZE, SIZE)
        full = jnp.where(mask, full, 0.0)
        by_column = jnp.sum(jnp.where(same, full, 0.0), axis=0, keepdims=True)
        squares = jnp.sum(jnp.where(mask, by_column, 0.0), axis=1, keepdims=True)
        norm = jnp.sqrt(squares) + EPSILON
        inverse = 1.0 / norm
        grams.append(full * (inverse * inverse))
        currents.append((rows / norm).astype(BF16))
    for sweep_index in range(ITERS):
        parts = [split(gram) for gram in grams]
        squared = [dot(part[0], part[0]) for part in parts]
        polynomials = [
            (COEF_B * part[0].astype(F32) + COEF_C * square).astype(BF16) for part, square in zip(parts, squared)
        ]
        if sweep_index + 1 < ITERS:
            lefts = [
                COEF_A * gram + (dot(poly, part[1]) + dot(poly, part[0]))
                for gram, poly, part in zip(grams, polynomials, parts)
            ]
        currents = [
            (COEF_A * current.astype(F32) + dot(poly, current)).astype(BF16)
            for current, poly in zip(currents, polynomials)
        ]
        if sweep_index + 1 < ITERS:
            parts = [split(left) for left in lefts]
            grams = [
                COEF_A * left + (dot(part[1], poly) + dot(part[0], poly))
                for left, poly, part in zip(lefts, polynomials, parts)
            ]
    factor = ROW_SCALE * (float(R) ** 0.5)
    first, second = [(current.astype(F32) * factor) for current in currents]
    tiles = [first[:, :LANES], first[:, LANES:], second]
    tiles = [tile.reshape(BR, 1, GROUP, LANES) for tile in tiles]
    out_ref[...] = jnp.concatenate(tiles, axis=1).astype(BF16)


def vmem_call(kernel, shape, dtype, count, flops):
    return pl.pallas_call(
        kernel,
        out_shape=jax.ShapeDtypeStruct(shape, dtype),
        in_specs=[pl.BlockSpec(memory_space=pltpu.VMEM)] * count,
        out_specs=pl.BlockSpec(memory_space=pltpu.VMEM),
        compiler_params=pltpu.CompilerParams(vmem_limit_bytes=4 << 20),
        cost_estimate=pl.CostEstimate(flops=flops, bytes_accessed=0, transcendentals=0),
    )


def owner_groups():
    chunks = C // 256
    return [[(row * 5 + 8) % BR * chunks + chunk for row in range(BR)] for chunk in range(chunks)]


def chunk_groups():
    chunks = C // 256
    return [[row * chunks + (chunk ^ 2) for chunk in range(chunks)] for row in range(BR)]


def gather_sum(gradients):
    groups = lax.axis_size("dp")
    mats, blocks, width = gradients.shape
    parts = gradients.astype(BF16).reshape(mats, groups, blocks // groups, width).swapaxes(0, 1)
    arrived = lax.all_to_all(parts, "dp", 0, 0, tiled=True)
    return jnp.sum(arrived.astype(F32), axis=0)


def shards(gradients, momentum):
    mats, local, width = momentum.shape
    count = mats * local
    summed = gather_sum(gradients[0])
    momentum_next = DECAY * momentum + summed
    nesterov = (summed + DECAY * momentum_next).astype(BF16).reshape(count, width)
    outgoing = pack(nesterov)
    rows = lax.all_to_all(outgoing, "shard", 0, 0, tiled=True, axis_index_groups=owner_groups())
    chunks = C // width
    parts = vmem_call(gram_kernel, (chunks, 2, BR, SIZE), F32, 1, 0)(rows)
    grams = lax.all_to_all(parts, "shard", 0, 0, tiled=True, axis_index_groups=chunk_groups())
    finished = vmem_call(sweep_kernel, rows.shape, BF16, 2, 0)(grams, rows)
    returned = lax.all_to_all(finished, "shard", 0, 0, tiled=True, axis_index_groups=owner_groups())
    return momentum_next, unpack(returned, count).reshape(momentum.shape)


def solution(mesh):
    placed = (P("dp", None, None, "shard"), P(None, "dp", "shard"))
    return jax.shard_map(
        shards,
        mesh=mesh,
        in_specs=placed,
        out_specs=(P(None, "dp", "shard"), P(None, "dp", "shard")),
        check_vma=False,
    )
```

```python
import jax
import jax.numpy as jnp
from jax import lax
from jax.experimental import pallas as pl
from jax.experimental.pallas import tpu as pltpu
from jax.sharding import PartitionSpec as P

R = 7168
C = 2048
ITERS = 5
BR = 16

COEF_A = 3.4445
COEF_B = -4.775
COEF_C = 2.0315
DECAY = 0.95
EPSILON = 1e-07
ROW_SCALE = 0.2

F32 = jnp.float32
BF16 = jnp.bfloat16
CORES = 2
LANES = 128
GROUP = 8
HALF = GROUP // 2
SIZE = BR * GROUP
REST = 3
SENT = 2 * (GROUP + REST)


def dot(a, b):
    return jnp.dot(a, b, preferred_element_type=F32)


def split(a):
    high = a.astype(BF16)
    return high, (a - high.astype(F32)).astype(BF16)


def pack(rows):
    owners = BR
    count, width = rows.shape
    first = owners * GROUP
    halves = rows[:first].reshape(owners, GROUP, 2, LANES).swapaxes(1, 2).reshape(owners, 2 * GROUP, LANES)
    others = jnp.pad(rows[first:], ((0, first + owners * REST - count), (0, 0)))
    others = others.reshape(owners, REST, 2, LANES).swapaxes(1, 2).reshape(owners, 2 * REST, LANES)
    return jnp.concatenate([halves, others], axis=1).reshape(owners, -1, 2, LANES)


def unpack(pairs, count):
    owners = BR
    first = owners * GROUP
    tiles = pairs.reshape(owners, -1, LANES)
    halves = tiles[:, : 2 * GROUP].reshape(owners, 2, GROUP, LANES).swapaxes(1, 2).reshape(first, 2 * LANES)
    others = tiles[:, 2 * GROUP :].reshape(owners, 2, REST, LANES).swapaxes(1, 2).reshape(-1, 2 * LANES)
    return jnp.concatenate([halves, others[: count - first]], axis=0)


def row_groups(rows_ref):
    wide = rows_ref[...].astype(F32)
    empty = jnp.zeros((HALF - REST, LANES), F32)
    tiles = [[], [], []]
    for row in range(BR):
        base = row * SENT
        tiles[0].append(wide[base : base + GROUP])
        tiles[1].append(wide[base + GROUP : base + 2 * GROUP])
        base += 2 * GROUP
        tiles[2] += [wide[base : base + REST], empty, wide[base + REST : base + 2 * REST], empty]
    tiles = [jnp.concatenate(tile, axis=0) for tile in tiles]
    return [jnp.concatenate(tiles[:2], axis=1), tiles[2]]


def same_slot():
    rows = lax.broadcasted_iota(jnp.int32, (SIZE, SIZE), 0)
    columns = lax.broadcasted_iota(jnp.int32, (SIZE, SIZE), 1)
    return rows % GROUP == columns % GROUP


def gram_kernel(rows_ref, gram_ref):
    mask = same_slot()
    parts = []
    for rows in row_groups(rows_ref):
        rows = rows.astype(BF16)
        full = lax.dot_general(rows, rows, (((1,), (1,)), ((), ())), preferred_element_type=F32)
        parts.append(jnp.sum(jnp.where(mask, full, 0.0).reshape(BR, GROUP, SIZE), axis=1))
    halves = parts[1]
    low_half = lax.broadcasted_iota(jnp.int32, halves.shape, 1) % GROUP < HALF
    halves = halves + jnp.where(low_half, pltpu.roll(halves, SIZE - HALF, 1), pltpu.roll(halves, HALF, 1))
    parts[1] = jnp.where(low_half[:GROUP], halves[:GROUP], halves[GROUP:])
    packed = jnp.concatenate(parts, axis=0)
    for peer in range(gram_ref.shape[0]):
        gram_ref[peer] = packed


def unfold(total, group):
    if group == 0:
        return total[:BR]
    folded = total[BR:]
    low_half = lax.broadcasted_iota(jnp.int32, folded.shape, 1) % GROUP < HALF
    upper = jnp.where(low_half, folded, pltpu.roll(folded, HALF, 1))
    lower = jnp.where(low_half, pltpu.roll(folded, SIZE - HALF, 1), folded)
    return jnp.concatenate([upper, lower], axis=0)


def sweep_kernel(grams_ref, rows_ref, momentum_ref, out_ref, momentum_out_ref, done):
    written = pltpu.make_async_copy(momentum_ref, momentum_out_ref, done)
    written.start()
    mask = same_slot()
    same = lax.broadcasted_iota(jnp.int32, (SIZE, SIZE), 0) == lax.broadcasted_iota(jnp.int32, (SIZE, SIZE), 1)
    total = jnp.sum(grams_ref[...], axis=0)
    grams = []
    currents = []
    for group, rows in enumerate(row_groups(rows_ref)):
        gram = unfold(total, group)
        full = jnp.broadcast_to(gram[:, None, :], (BR, GROUP, SIZE)).reshape(SIZE, SIZE)
        full = jnp.where(mask, full, 0.0)
        by_column = jnp.sum(jnp.where(same, full, 0.0), axis=0, keepdims=True)
        squares = jnp.sum(jnp.where(mask, by_column, 0.0), axis=1, keepdims=True)
        norm = jnp.sqrt(squares) + EPSILON
        inverse = 1.0 / norm
        grams.append(full * (inverse * inverse))
        currents.append((rows / norm).astype(BF16))
    for sweep_index in range(ITERS):
        parts = [split(gram) for gram in grams]
        squared = [dot(part[0], part[0]) for part in parts]
        polynomials = [
            (COEF_B * part[0].astype(F32) + COEF_C * square).astype(BF16) for part, square in zip(parts, squared)
        ]
        if sweep_index + 1 < ITERS:
            lefts = [
                COEF_A * gram + (dot(poly, part[1]) + dot(poly, part[0]))
                for gram, poly, part in zip(grams, polynomials, parts)
            ]
        currents = [
            (COEF_A * current.astype(F32) + dot(poly, current)).astype(BF16)
            for current, poly in zip(currents, polynomials)
        ]
        if sweep_index + 1 < ITERS:
            parts = [split(left) for left in lefts]
            grams = [
                COEF_A * left + (dot(part[1], poly) + dot(part[0], poly))
                for left, poly, part in zip(lefts, polynomials, parts)
            ]
    factor = ROW_SCALE * (float(R) ** 0.5)
    first, second = [(current.astype(F32) * factor) for current in currents]
    pieces = []
    for row in range(BR):
        base = row * GROUP
        pieces += [first[base : base + GROUP, :LANES], first[base : base + GROUP, LANES:]]
        pieces += [second[base : base + REST], second[base + HALF : base + HALF + REST]]
    out_ref[...] = jnp.concatenate(pieces, axis=0).astype(BF16)
    written.wait()


def vmem_call(kernel, shape, dtype, count, flops):
    return pl.pallas_call(
        kernel,
        out_shape=jax.ShapeDtypeStruct(shape, dtype),
        in_specs=[pl.BlockSpec(memory_space=pltpu.VMEM)] * count,
        out_specs=pl.BlockSpec(memory_space=pltpu.VMEM),
        compiler_params=pltpu.CompilerParams(vmem_limit_bytes=4 << 20),
        cost_estimate=pl.CostEstimate(flops=flops, bytes_accessed=0, transcendentals=0),
    )


def owner_groups():
    chunks = C // 256
    return [[(row * 5 + 8) % BR * chunks + chunk for row in range(BR)] for chunk in range(chunks)]


def chunk_groups():
    chunks = C // 256
    return [[row * chunks + (chunk ^ 2) for chunk in range(chunks)] for row in range(BR)]


def gather_sum(gradients):
    groups = lax.axis_size("dp")
    mats, blocks, width = gradients.shape
    core = lax.axis_index("dp") % CORES
    parts = gradients.reshape(mats, groups // CORES, CORES, blocks // groups, width)
    sent = lax.dynamic_index_in_dim(parts, 1 - core, 2, keepdims=False).astype(BF16)
    arrived = lax.ppermute(sent, "dp", [(i, i ^ 1) for i in range(groups)])
    own = lax.optimization_barrier(lax.dynamic_index_in_dim(parts, core, 2, keepdims=False))
    pair = (own + arrived.astype(F32)).astype(BF16).swapaxes(0, 1)
    chips = [[chip * CORES + side for chip in range(groups // CORES)] for side in range(CORES)]
    arrived = lax.all_to_all(pair, "dp", 0, 0, tiled=True, axis_index_groups=chips)
    return jnp.sum(arrived.astype(F32), axis=0)


def shards(gradients, momentum):
    mats, local, width = momentum.shape
    count = mats * local
    summed = gather_sum(gradients[0])
    momentum_next = DECAY * momentum + summed
    nesterov = (summed + DECAY * momentum_next).astype(BF16).reshape(count, width)
    outgoing = pack(nesterov)
    rows = lax.all_to_all(outgoing, "shard", 0, 0, tiled=True, axis_index_groups=owner_groups())
    rows = rows.reshape(BR * SENT, LANES)
    chunks = C // width
    parts = vmem_call(gram_kernel, (chunks, BR + GROUP, SIZE), F32, 1, 0)(rows)
    grams = lax.all_to_all(parts, "shard", 0, 0, tiled=True, axis_index_groups=chunk_groups())
    finished, momentum_out = pl.pallas_call(
        sweep_kernel,
        out_shape=[
            jax.ShapeDtypeStruct(rows.shape, BF16),
            jax.ShapeDtypeStruct(momentum.shape, F32),
        ],
        in_specs=[pl.BlockSpec(memory_space=pltpu.VMEM)] * 3,
        out_specs=[pl.BlockSpec(memory_space=pltpu.VMEM), pl.BlockSpec(memory_space=pl.ANY)],
        scratch_shapes=[pltpu.SemaphoreType.DMA],
        compiler_params=pltpu.CompilerParams(vmem_limit_bytes=4 << 20),
    )(grams, rows, momentum_next)
    finished = finished.reshape(outgoing.shape)
    returned = lax.all_to_all(finished, "shard", 0, 0, tiled=True, axis_index_groups=owner_groups())
    return momentum_out, unpack(returned, count).reshape(momentum.shape)


def solution(mesh):
    placed = (P("dp", None, None, "shard"), P(None, "dp", "shard"))
    return jax.shard_map(
        shards,
        mesh=mesh,
        in_specs=placed,
        out_specs=(P(None, "dp", "shard"), P(None, "dp", "shard")),
        check_vma=False,
    )
```

```python
import jax
import jax.numpy as jnp
from jax import lax
from jax.experimental import pallas as pl
from jax.experimental.pallas import tpu as pltpu
from jax.sharding import PartitionSpec as P

R = 7168
C = 2048
ITERS = 5
BR = 16

COEF_A = 3.4445
COEF_B = -4.775
COEF_C = 2.0315
DECAY = 0.95
EPSILON = 1e-07
ROW_SCALE = 0.2

F32 = jnp.float32
BF16 = jnp.bfloat16
CORES = 2
LANES = 128
GROUP = 8
HALF = GROUP // 2
SIZE = BR * GROUP
REST = 3
SENT = 2 * (GROUP + REST)


def dot(a, b):
    return jnp.dot(a, b, preferred_element_type=F32)


def split(a):
    high = a.astype(BF16)
    return high, (a - high.astype(F32)).astype(BF16)


def pack(rows):
    owners = BR
    count, width = rows.shape
    first = owners * GROUP
    halves = rows[:first].reshape(owners, GROUP, 2, LANES).swapaxes(1, 2).reshape(owners, 2 * GROUP, LANES)
    others = jnp.pad(rows[first:], ((0, first + owners * REST - count), (0, 0)))
    others = others.reshape(owners, REST, 2, LANES).swapaxes(1, 2).reshape(owners, 2 * REST, LANES)
    return jnp.concatenate([halves, others], axis=1).reshape(owners, -1, 2, LANES)


def unpack(pairs, count):
    owners = BR
    first = owners * GROUP
    tiles = pairs.reshape(owners, -1, LANES)
    halves = tiles[:, : 2 * GROUP].reshape(owners, 2, GROUP, LANES).swapaxes(1, 2).reshape(first, 2 * LANES)
    others = tiles[:, 2 * GROUP :].reshape(owners, 2, REST, LANES).swapaxes(1, 2).reshape(-1, 2 * LANES)
    return jnp.concatenate([halves, others[: count - first]], axis=0)


def row_groups(rows_ref):
    wide = rows_ref[...].astype(F32)
    empty = jnp.zeros((HALF - REST, LANES), F32)
    tiles = [[], [], []]
    for row in range(BR):
        base = row * SENT
        tiles[0].append(wide[base : base + GROUP])
        tiles[1].append(wide[base + GROUP : base + 2 * GROUP])
        base += 2 * GROUP
        tiles[2] += [wide[base : base + REST], empty, wide[base + REST : base + 2 * REST], empty]
    tiles = [jnp.concatenate(tile, axis=0) for tile in tiles]
    return [jnp.concatenate(tiles[:2], axis=1), tiles[2]]


def same_slot():
    rows = lax.broadcasted_iota(jnp.int32, (SIZE, SIZE), 0)
    columns = lax.broadcasted_iota(jnp.int32, (SIZE, SIZE), 1)
    return rows % GROUP == columns % GROUP


def gram_kernel(rows_ref, gram_ref):
    mask = same_slot()
    parts = []
    for rows in row_groups(rows_ref):
        rows = rows.astype(BF16)
        full = lax.dot_general(rows, rows, (((1,), (1,)), ((), ())), preferred_element_type=F32)
        parts.append(jnp.sum(jnp.where(mask, full, 0.0).reshape(BR, GROUP, SIZE), axis=1))
    halves = parts[1]
    low_half = lax.broadcasted_iota(jnp.int32, halves.shape, 1) % GROUP < HALF
    halves = halves + jnp.where(low_half, pltpu.roll(halves, SIZE - HALF, 1), pltpu.roll(halves, HALF, 1))
    parts[1] = jnp.where(low_half[:GROUP], halves[:GROUP], halves[GROUP:])
    packed = jnp.concatenate(parts, axis=0)
    for peer in range(gram_ref.shape[0]):
        gram_ref[peer] = packed


def unfold(total, group):
    if group == 0:
        return total[:BR]
    folded = total[BR:]
    low_half = lax.broadcasted_iota(jnp.int32, folded.shape, 1) % GROUP < HALF
    upper = jnp.where(low_half, folded, pltpu.roll(folded, HALF, 1))
    lower = jnp.where(low_half, pltpu.roll(folded, SIZE - HALF, 1), folded)
    return jnp.concatenate([upper, lower], axis=0)


def sweep_kernel(grams_ref, rows_ref, momentum_ref, out_ref, momentum_out_ref, done):
    written = pltpu.make_async_copy(momentum_ref, momentum_out_ref, done)
    written.start()
    mask = same_slot()
    same = lax.broadcasted_iota(jnp.int32, (SIZE, SIZE), 0) == lax.broadcasted_iota(jnp.int32, (SIZE, SIZE), 1)
    total = jnp.sum(grams_ref[...], axis=0)
    grams = []
    currents = []
    for group, rows in enumerate(row_groups(rows_ref)):
        gram = unfold(total, group)
        full = jnp.broadcast_to(gram[:, None, :], (BR, GROUP, SIZE)).reshape(SIZE, SIZE)
        full = jnp.where(mask, full, 0.0)
        by_column = jnp.sum(jnp.where(same, full, 0.0), axis=0, keepdims=True)
        squares = jnp.sum(jnp.where(mask, by_column, 0.0), axis=1, keepdims=True)
        norm = jnp.sqrt(squares) + EPSILON
        inverse = 1.0 / norm
        grams.append(full * (inverse * inverse))
        currents.append((rows / norm).astype(BF16))
    for sweep_index in range(ITERS):
        parts = [split(gram) for gram in grams]
        squared = [dot(part[0], part[0]) for part in parts]
        polynomials = [
            (COEF_B * part[0].astype(F32) + COEF_C * square).astype(BF16) for part, square in zip(parts, squared)
        ]
        if sweep_index + 1 < ITERS:
            lefts = [
                COEF_A * gram + dot(jnp.concatenate([poly, poly], axis=1), jnp.concatenate(part, axis=0))
                for gram, poly, part in zip(grams, polynomials, parts)
            ]
        currents = [
            (COEF_A * current.astype(F32) + dot(poly, current)).astype(BF16)
            for current, poly in zip(currents, polynomials)
        ]
        if sweep_index + 1 < ITERS:
            parts = [split(left) for left in lefts]
            grams = [
                COEF_A * left + dot(jnp.concatenate(part, axis=1), jnp.concatenate([poly, poly], axis=0))
                for left, poly, part in zip(lefts, polynomials, parts)
            ]
    factor = ROW_SCALE * (float(R) ** 0.5)
    first, second = [(current.astype(F32) * factor) for current in currents]
    pieces = []
    for row in range(BR):
        base = row * GROUP
        pieces += [first[base : base + GROUP, :LANES], first[base : base + GROUP, LANES:]]
        pieces += [second[base : base + REST], second[base + HALF : base + HALF + REST]]
    out_ref[...] = jnp.concatenate(pieces, axis=0).astype(BF16)
    written.wait()


def vmem_call(kernel, shape, dtype, count, flops):
    return pl.pallas_call(
        kernel,
        out_shape=jax.ShapeDtypeStruct(shape, dtype),
        in_specs=[pl.BlockSpec(memory_space=pltpu.VMEM)] * count,
        out_specs=pl.BlockSpec(memory_space=pltpu.VMEM),
        compiler_params=pltpu.CompilerParams(vmem_limit_bytes=4 << 20),
        cost_estimate=pl.CostEstimate(flops=flops, bytes_accessed=0, transcendentals=0),
    )


def owner_groups():
    chunks = C // 256
    return [[(row * 5 + 8) % BR * chunks + chunk for row in range(BR)] for chunk in range(chunks)]


def chunk_groups():
    chunks = C // 256
    return [[row * chunks + (chunk ^ 2) for chunk in range(chunks)] for row in range(BR)]


def gather_sum(gradients):
    groups = lax.axis_size("dp")
    mats, blocks, width = gradients.shape
    core = lax.axis_index("dp") % CORES
    parts = gradients.reshape(mats, groups // CORES, CORES, blocks // groups, width)
    sent = lax.dynamic_index_in_dim(parts, 1 - core, 2, keepdims=False).astype(BF16)
    arrived = lax.ppermute(sent, "dp", [(i, i ^ 1) for i in range(groups)])
    _, again = lax.optimization_barrier((sent, parts))
    own = lax.optimization_barrier(lax.dynamic_index_in_dim(again, core, 2, keepdims=False).astype(BF16))
    pair = (own.astype(F32) + arrived.astype(F32)).astype(BF16).swapaxes(0, 1)
    chips = [[chip * CORES + side for chip in range(groups // CORES)] for side in range(CORES)]
    arrived = lax.all_to_all(pair, "dp", 0, 0, tiled=True, axis_index_groups=chips)
    return jnp.sum(arrived.astype(F32), axis=0)


def shards(gradients, momentum):
    mats, local, width = momentum.shape
    count = mats * local
    summed = gather_sum(gradients[0])
    momentum_next = DECAY * momentum + summed
    nesterov = (summed + DECAY * momentum_next).astype(BF16).reshape(count, width)
    outgoing = pack(nesterov)
    rows = lax.all_to_all(outgoing, "shard", 0, 0, tiled=True, axis_index_groups=owner_groups())
    rows = rows.reshape(BR * SENT, LANES)
    chunks = C // width
    parts = vmem_call(gram_kernel, (chunks, BR + GROUP, SIZE), F32, 1, 0)(rows)
    grams = lax.all_to_all(parts, "shard", 0, 0, tiled=True, axis_index_groups=chunk_groups())
    finished, momentum_out = pl.pallas_call(
        sweep_kernel,
        out_shape=[
            jax.ShapeDtypeStruct(rows.shape, BF16),
            jax.ShapeDtypeStruct(momentum.shape, F32),
        ],
        in_specs=[pl.BlockSpec(memory_space=pltpu.VMEM)] * 3,
        out_specs=[pl.BlockSpec(memory_space=pltpu.VMEM), pl.BlockSpec(memory_space=pl.ANY)],
        scratch_shapes=[pltpu.SemaphoreType.DMA],
        compiler_params=pltpu.CompilerParams(vmem_limit_bytes=4 << 20),
    )(grams, rows, momentum_next)
    finished = finished.reshape(outgoing.shape)
    returned = lax.all_to_all(finished, "shard", 0, 0, tiled=True, axis_index_groups=owner_groups())
    return momentum_out, unpack(returned, count).reshape(momentum.shape)


def solution(mesh):
    placed = (P("dp", None, None, "shard"), P(None, "dp", "shard"))
    return jax.shard_map(
        shards,
        mesh=mesh,
        in_specs=placed,
        out_specs=(P(None, "dp", "shard"), P(None, "dp", "shard")),
        check_vma=False,
    )
```

```python
import jax
import jax.numpy as jnp
from jax import lax
from jax.experimental import pallas as pl
from jax.experimental.pallas import tpu as pltpu
from jax.sharding import PartitionSpec as P

R = 7168
C = 2048
ITERS = 5
BR = 16

COEF_A = 3.4445
COEF_B = -4.775
COEF_C = 2.0315
DECAY = 0.95
EPSILON = 1e-07
ROW_SCALE = 0.2

F32 = jnp.float32
BF16 = jnp.bfloat16
CORES = 2
LANES = 128
GROUP = 8
HALF = GROUP // 2
SIZE = BR * GROUP
REST = 3
SENT = 2 * (GROUP + REST)


def dot(a, b):
    return jnp.dot(a, b, preferred_element_type=F32)


def split(a):
    high = a.astype(BF16)
    return high, (a - high.astype(F32)).astype(BF16)


def pack(rows):
    owners = BR
    count, width = rows.shape
    first = owners * GROUP
    halves = rows[:first].reshape(owners, GROUP, 2, LANES).swapaxes(1, 2).reshape(owners, 2 * GROUP, LANES)
    others = jnp.pad(rows[first:], ((0, first + owners * REST - count), (0, 0)))
    others = others.reshape(owners, REST, 2, LANES).swapaxes(1, 2).reshape(owners, 2 * REST, LANES)
    return jnp.concatenate([halves, others], axis=1).reshape(owners, -1, 2, LANES)


def unpack(pairs, count):
    owners = BR
    first = owners * GROUP
    tiles = pairs.reshape(owners, -1, LANES)
    halves = tiles[:, : 2 * GROUP].reshape(owners, 2, GROUP, LANES).swapaxes(1, 2).reshape(first, 2 * LANES)
    others = tiles[:, 2 * GROUP :].reshape(owners, 2, REST, LANES).swapaxes(1, 2).reshape(-1, 2 * LANES)
    return jnp.concatenate([halves, others[: count - first]], axis=0)


def row_groups(rows_ref):
    wide = rows_ref[...].astype(F32)
    empty = jnp.zeros((HALF - REST, LANES), F32)
    tiles = [[], [], []]
    for row in range(BR):
        base = row * SENT
        tiles[0].append(wide[base : base + GROUP])
        tiles[1].append(wide[base + GROUP : base + 2 * GROUP])
        base += 2 * GROUP
        tiles[2] += [wide[base : base + REST], empty, wide[base + REST : base + 2 * REST], empty]
    tiles = [jnp.concatenate(tile, axis=0) for tile in tiles]
    return [jnp.concatenate(tiles[:2], axis=1), tiles[2]]


def same_slot():
    rows = lax.broadcasted_iota(jnp.int32, (SIZE, SIZE), 0)
    columns = lax.broadcasted_iota(jnp.int32, (SIZE, SIZE), 1)
    return rows % GROUP == columns % GROUP


def gram_kernel(rows_ref, gram_ref):
    mask = same_slot()
    parts = []
    for rows in row_groups(rows_ref):
        rows = rows.astype(BF16)
        full = lax.dot_general(rows, rows, (((1,), (1,)), ((), ())), preferred_element_type=F32)
        parts.append(jnp.sum(jnp.where(mask, full, 0.0).reshape(BR, GROUP, SIZE), axis=1))
    halves = parts[1]
    low_half = lax.broadcasted_iota(jnp.int32, halves.shape, 1) % GROUP < HALF
    halves = halves + jnp.where(low_half, pltpu.roll(halves, SIZE - HALF, 1), pltpu.roll(halves, HALF, 1))
    parts[1] = jnp.where(low_half[:GROUP], halves[:GROUP], halves[GROUP:])
    packed = jnp.concatenate(parts, axis=0)
    for peer in range(gram_ref.shape[0]):
        gram_ref[peer] = packed


def unfold(total, group):
    if group == 0:
        return total[:BR]
    folded = total[BR:]
    low_half = lax.broadcasted_iota(jnp.int32, folded.shape, 1) % GROUP < HALF
    upper = jnp.where(low_half, folded, pltpu.roll(folded, HALF, 1))
    lower = jnp.where(low_half, pltpu.roll(folded, SIZE - HALF, 1), folded)
    return jnp.concatenate([upper, lower], axis=0)


def sweep_kernel(grams_ref, rows_ref, momentum_ref, out_ref, momentum_out_ref, done):
    written = pltpu.make_async_copy(momentum_ref, momentum_out_ref, done)
    written.start()
    mask = same_slot()
    same = lax.broadcasted_iota(jnp.int32, (SIZE, SIZE), 0) == lax.broadcasted_iota(jnp.int32, (SIZE, SIZE), 1)
    total = jnp.sum(grams_ref[...], axis=0)
    grams = []
    currents = []
    for group, rows in enumerate(row_groups(rows_ref)):
        gram = unfold(total, group)
        full = jnp.broadcast_to(gram[:, None, :], (BR, GROUP, SIZE)).reshape(SIZE, SIZE)
        full = jnp.where(mask, full, 0.0)
        by_column = jnp.sum(jnp.where(same, full, 0.0), axis=0, keepdims=True)
        squares = jnp.sum(jnp.where(mask, by_column, 0.0), axis=1, keepdims=True)
        norm = jnp.sqrt(squares) + EPSILON
        inverse = 1.0 / norm
        grams.append(full * (inverse * inverse))
        currents.append((rows / norm).astype(BF16))
    for sweep_index in range(ITERS):
        parts = [split(gram) for gram in grams]
        squared = [dot(part[0], part[0]) for part in parts]
        polynomials = [
            (COEF_B * part[0].astype(F32) + COEF_C * square).astype(BF16) for part, square in zip(parts, squared)
        ]
        if sweep_index + 1 < ITERS:
            lefts = [
                COEF_A * gram + dot(jnp.concatenate([poly, poly], axis=1), jnp.concatenate(part, axis=0))
                for gram, poly, part in zip(grams, polynomials, parts)
            ]
        currents = [
            (COEF_A * current.astype(F32) + dot(poly, current)).astype(BF16)
            for current, poly in zip(currents, polynomials)
        ]
        if sweep_index + 1 < ITERS:
            parts = [split(left) for left in lefts]
            grams = [
                COEF_A * left + dot(jnp.concatenate(part, axis=1), jnp.concatenate([poly, poly], axis=0))
                for left, poly, part in zip(lefts, polynomials, parts)
            ]
    factor = ROW_SCALE * (float(R) ** 0.5)
    first, second = [(current.astype(F32) * factor) for current in currents]
    pieces = []
    for row in range(BR):
        base = row * GROUP
        pieces += [first[base : base + GROUP, :LANES], first[base : base + GROUP, LANES:]]
        pieces += [second[base : base + REST], second[base + HALF : base + HALF + REST]]
    out_ref[...] = jnp.concatenate(pieces, axis=0).astype(BF16)
    written.wait()


def vmem_call(kernel, shape, dtype, count, flops):
    return pl.pallas_call(
        kernel,
        out_shape=jax.ShapeDtypeStruct(shape, dtype),
        in_specs=[pl.BlockSpec(memory_space=pltpu.VMEM)] * count,
        out_specs=pl.BlockSpec(memory_space=pltpu.VMEM),
        compiler_params=pltpu.CompilerParams(vmem_limit_bytes=4 << 20),
        cost_estimate=pl.CostEstimate(flops=flops, bytes_accessed=0, transcendentals=0),
    )


def owner_groups():
    chunks = C // 256
    return [[(row * 5 + 8) % BR * chunks + chunk for row in range(BR)] for chunk in range(chunks)]


def chunk_groups():
    chunks = C // 256
    return [[row * chunks + (chunk ^ 2) for chunk in range(chunks)] for row in range(BR)]


def gather_sum(gradients):
    groups = lax.axis_size("dp")
    mats, blocks, width = gradients.shape
    core = lax.axis_index("dp") % CORES
    parts = gradients.reshape(mats, groups // CORES, CORES, blocks // groups, width)
    sent = lax.dynamic_index_in_dim(parts, 1 - core, 2, keepdims=False).astype(BF16)
    arrived = lax.ppermute(sent, "dp", [(i, i ^ 1) for i in range(groups)])
    _, again = lax.optimization_barrier((sent, parts))
    own = lax.optimization_barrier(lax.dynamic_index_in_dim(again, core, 2, keepdims=False).astype(BF16))
    pair = (own.astype(F32) + arrived.astype(F32)).astype(BF16)
    order = (2, 1, 0, 3)
    pair = jnp.stack([pair[:, chip] for chip in order])
    chips = [[chip * CORES + side for chip in order] for side in range(CORES)]
    arrived = lax.all_to_all(pair, "dp", 0, 0, tiled=True, axis_index_groups=chips)
    return jnp.sum(arrived.astype(F32), axis=0)


def shards(gradients, momentum):
    mats, local, width = momentum.shape
    count = mats * local
    summed = gather_sum(gradients[0])
    momentum_next = DECAY * momentum + summed
    nesterov = (summed + DECAY * momentum_next).astype(BF16).reshape(count, width)
    outgoing = pack(nesterov)
    rows = lax.all_to_all(outgoing, "shard", 0, 0, tiled=True, axis_index_groups=owner_groups())
    rows = rows.reshape(BR * SENT, LANES)
    chunks = C // width
    parts = vmem_call(gram_kernel, (chunks, BR + GROUP, SIZE), F32, 1, 0)(rows)
    grams = lax.all_to_all(parts, "shard", 0, 0, tiled=True, axis_index_groups=chunk_groups())
    finished, momentum_out = pl.pallas_call(
        sweep_kernel,
        out_shape=[
            jax.ShapeDtypeStruct(rows.shape, BF16),
            jax.ShapeDtypeStruct(momentum.shape, F32),
        ],
        in_specs=[pl.BlockSpec(memory_space=pltpu.VMEM)] * 3,
        out_specs=[pl.BlockSpec(memory_space=pltpu.VMEM), pl.BlockSpec(memory_space=pl.ANY)],
        scratch_shapes=[pltpu.SemaphoreType.DMA],
        compiler_params=pltpu.CompilerParams(vmem_limit_bytes=4 << 20),
    )(grams, rows, momentum_next)
    finished = finished.reshape(outgoing.shape)
    returned = lax.all_to_all(finished, "shard", 0, 0, tiled=True, axis_index_groups=owner_groups())
    return momentum_out, unpack(returned, count).reshape(momentum.shape)


def solution(mesh):
    placed = (P("dp", None, None, "shard"), P(None, "dp", "shard"))
    return jax.shard_map(
        shards,
        mesh=mesh,
        in_specs=placed,
        out_specs=(P(None, "dp", "shard"), P(None, "dp", "shard")),
        check_vma=False,
    )
```

```python
import jax
import jax.numpy as jnp
from jax import lax
from jax.experimental import pallas as pl
from jax.experimental.pallas import tpu as pltpu
from jax.sharding import PartitionSpec as P

R = 7168
C = 2048
ITERS = 5
BR = 16

COEF_A = 3.4445
COEF_B = -4.775
COEF_C = 2.0315
DECAY = 0.95
EPSILON = 1e-07
ROW_SCALE = 0.2

F32 = jnp.float32
BF16 = jnp.bfloat16
CORES = 2
LANES = 128
GROUP = 8
HALF = GROUP // 2
SIZE = BR * GROUP
REST = 3
SENT = 2 * (GROUP + REST)


def dot(a, b):
    return jnp.dot(a, b, preferred_element_type=F32)


def split(a):
    high = a.astype(BF16)
    return high, (a - high.astype(F32)).astype(BF16)


def pack(rows):
    owners = BR
    count, width = rows.shape
    first = owners * GROUP
    halves = rows[:first].reshape(owners, GROUP, 2, LANES).swapaxes(1, 2).reshape(owners, 2 * GROUP, LANES)
    others = jnp.pad(rows[first:], ((0, first + owners * REST - count), (0, 0)))
    others = others.reshape(owners, REST, 2, LANES).swapaxes(1, 2).reshape(owners, 2 * REST, LANES)
    return jnp.concatenate([halves, others], axis=1).reshape(owners, -1, 2, LANES)


def unpack(pairs, count):
    owners = BR
    first = owners * GROUP
    tiles = pairs.reshape(owners, -1, LANES)
    halves = tiles[:, : 2 * GROUP].reshape(owners, 2, GROUP, LANES).swapaxes(1, 2).reshape(first, 2 * LANES)
    others = tiles[:, 2 * GROUP :].reshape(owners, 2, REST, LANES).swapaxes(1, 2).reshape(-1, 2 * LANES)
    return jnp.concatenate([halves, others[: count - first]], axis=0)


def row_groups(rows_ref):
    wide = rows_ref[...].astype(F32)
    empty = jnp.zeros((HALF - REST, LANES), F32)
    tiles = [[], [], []]
    for row in range(BR):
        base = row * SENT
        tiles[0].append(wide[base : base + GROUP])
        tiles[1].append(wide[base + GROUP : base + 2 * GROUP])
        base += 2 * GROUP
        tiles[2] += [wide[base : base + REST], empty, wide[base + REST : base + 2 * REST], empty]
    tiles = [jnp.concatenate(tile, axis=0) for tile in tiles]
    return [jnp.concatenate(tiles[:2], axis=1), tiles[2]]


def same_slot():
    rows = lax.broadcasted_iota(jnp.int32, (SIZE, SIZE), 0)
    columns = lax.broadcasted_iota(jnp.int32, (SIZE, SIZE), 1)
    return rows % GROUP == columns % GROUP


def gram_kernel(rows_ref, gram_ref):
    mask = same_slot()
    parts = []
    for rows in row_groups(rows_ref):
        rows = rows.astype(BF16)
        full = lax.dot_general(rows, rows, (((1,), (1,)), ((), ())), preferred_element_type=F32)
        parts.append(jnp.sum(jnp.where(mask, full, 0.0).reshape(BR, GROUP, SIZE), axis=1))
    halves = parts[1]
    low_half = lax.broadcasted_iota(jnp.int32, halves.shape, 1) % GROUP < HALF
    halves = halves + jnp.where(low_half, pltpu.roll(halves, SIZE - HALF, 1), pltpu.roll(halves, HALF, 1))
    parts[1] = jnp.where(low_half[:GROUP], halves[:GROUP], halves[GROUP:])
    packed = jnp.concatenate(parts, axis=0)
    for peer in range(gram_ref.shape[0]):
        gram_ref[peer] = packed


def unfold(total, group):
    if group == 0:
        return total[:BR]
    folded = total[BR:]
    low_half = lax.broadcasted_iota(jnp.int32, folded.shape, 1) % GROUP < HALF
    upper = jnp.where(low_half, folded, pltpu.roll(folded, HALF, 1))
    lower = jnp.where(low_half, pltpu.roll(folded, SIZE - HALF, 1), folded)
    return jnp.concatenate([upper, lower], axis=0)


def sweep_kernel(grams_ref, rows_ref, momentum_ref, out_ref, momentum_out_ref, done):
    written = pltpu.make_async_copy(momentum_ref, momentum_out_ref, done)
    written.start()
    mask = same_slot()
    same = lax.broadcasted_iota(jnp.int32, (SIZE, SIZE), 0) == lax.broadcasted_iota(jnp.int32, (SIZE, SIZE), 1)
    total = jnp.sum(grams_ref[...], axis=0)
    grams = []
    currents = []
    for group, rows in enumerate(row_groups(rows_ref)):
        gram = unfold(total, group)
        full = jnp.broadcast_to(gram[:, None, :], (BR, GROUP, SIZE)).reshape(SIZE, SIZE)
        full = jnp.where(mask, full, 0.0)
        by_column = jnp.sum(jnp.where(same, full, 0.0), axis=0, keepdims=True)
        squares = jnp.sum(jnp.where(mask, by_column, 0.0), axis=1, keepdims=True)
        norm = jnp.sqrt(squares) + EPSILON
        inverse = 1.0 / norm
        grams.append(full * (inverse * inverse))
        currents.append((rows / norm).astype(BF16))
    for sweep_index in range(ITERS):
        parts = [split(gram) for gram in grams]
        squared = [dot(part[0], part[0]) for part in parts]
        polynomials = [
            (COEF_B * part[0].astype(F32) + COEF_C * square).astype(BF16) for part, square in zip(parts, squared)
        ]
        if sweep_index + 1 < ITERS:
            lefts = [
                COEF_A * gram + dot(jnp.concatenate([poly, poly], axis=1), jnp.concatenate(part, axis=0))
                for gram, poly, part in zip(grams, polynomials, parts)
            ]
        currents = [
            (COEF_A * current.astype(F32) + dot(poly, current)).astype(BF16)
            for current, poly in zip(currents, polynomials)
        ]
        if sweep_index + 1 < ITERS:
            parts = [split(left) for left in lefts]
            grams = [
                COEF_A * left + dot(jnp.concatenate(part, axis=1), jnp.concatenate([poly, poly], axis=0))
                for left, poly, part in zip(lefts, polynomials, parts)
            ]
    factor = ROW_SCALE * (float(R) ** 0.5)
    first, second = [(current.astype(F32) * factor) for current in currents]
    pieces = []
    for row in range(BR):
        base = row * GROUP
        pieces += [first[base : base + GROUP, :LANES], first[base : base + GROUP, LANES:]]
        pieces += [second[base : base + REST], second[base + HALF : base + HALF + REST]]
    out_ref[...] = jnp.concatenate(pieces, axis=0).astype(BF16)
    written.wait()


def vmem_call(kernel, shape, dtype, count, flops):
    return pl.pallas_call(
        kernel,
        out_shape=jax.ShapeDtypeStruct(shape, dtype),
        in_specs=[pl.BlockSpec(memory_space=pltpu.VMEM)] * count,
        out_specs=pl.BlockSpec(memory_space=pltpu.VMEM),
        compiler_params=pltpu.CompilerParams(vmem_limit_bytes=4 << 20),
        cost_estimate=pl.CostEstimate(flops=flops, bytes_accessed=0, transcendentals=0),
    )


def owner_groups():
    chunks = C // 256
    return [[(row * 5 + 8) % BR * chunks + chunk for row in range(BR)] for chunk in range(chunks)]


def chunk_groups():
    chunks = C // 256
    return [[row * chunks + (chunk ^ 2) for chunk in range(chunks)] for row in range(BR)]


def gather_sum(gradients):
    groups = lax.axis_size("dp")
    mats, blocks, width = gradients.shape
    core = lax.axis_index("dp") % CORES
    parts = gradients.reshape(mats, groups // CORES, CORES, blocks // groups, width)
    sent = lax.dynamic_index_in_dim(parts, 1 - core, 2, keepdims=False).astype(BF16)
    arrived = lax.ppermute(sent, "dp", [(i, i ^ 1) for i in range(groups)])
    _, again = lax.optimization_barrier((sent, gradients))
    again = again.reshape(parts.shape)
    own = lax.optimization_barrier(lax.dynamic_index_in_dim(again, core, 2, keepdims=False).astype(BF16))
    pair = (own.astype(F32) + arrived.astype(F32)).astype(BF16)
    order = (2, 1, 0, 3)
    pair = jnp.stack([pair[:, chip] for chip in order])
    chips = [[chip * CORES + side for chip in order] for side in range(CORES)]
    arrived = lax.all_to_all(pair, "dp", 0, 0, tiled=True, axis_index_groups=chips)
    return jnp.sum(arrived.astype(F32), axis=0)


def shards(gradients, momentum):
    mats, local, width = momentum.shape
    count = mats * local
    summed = gather_sum(gradients[0])
    momentum_next = DECAY * momentum + summed
    nesterov = (summed + DECAY * momentum_next).astype(BF16).reshape(count, width)
    outgoing = pack(nesterov)
    rows = lax.all_to_all(outgoing, "shard", 0, 0, tiled=True, axis_index_groups=owner_groups())
    rows = rows.reshape(BR * SENT, LANES)
    chunks = C // width
    parts = vmem_call(gram_kernel, (chunks, BR + GROUP, SIZE), F32, 1, 0)(rows)
    grams = lax.all_to_all(parts, "shard", 0, 0, tiled=True, axis_index_groups=chunk_groups())
    finished, momentum_out = pl.pallas_call(
        sweep_kernel,
        out_shape=[
            jax.ShapeDtypeStruct(rows.shape, BF16),
            jax.ShapeDtypeStruct(momentum.shape, F32),
        ],
        in_specs=[pl.BlockSpec(memory_space=pltpu.VMEM)] * 3,
        out_specs=[pl.BlockSpec(memory_space=pltpu.VMEM), pl.BlockSpec(memory_space=pl.ANY)],
        scratch_shapes=[pltpu.SemaphoreType.DMA],
        compiler_params=pltpu.CompilerParams(vmem_limit_bytes=4 << 20),
    )(grams, rows, momentum_next)
    finished = finished.reshape(outgoing.shape)
    returned = lax.all_to_all(finished, "shard", 0, 0, tiled=True, axis_index_groups=owner_groups())
    return momentum_out, unpack(returned, count).reshape(momentum.shape)


def solution(mesh):
    placed = (P("dp", None, None, "shard"), P(None, "dp", "shard"))
    return jax.shard_map(
        shards,
        mesh=mesh,
        in_specs=placed,
        out_specs=(P(None, "dp", "shard"), P(None, "dp", "shard")),
        check_vma=False,
    )
```

```python
import jax
import jax.numpy as jnp
from jax import lax
from jax.experimental import pallas as pl
from jax.experimental.pallas import tpu as pltpu
from jax.sharding import PartitionSpec as P

R = 7168
C = 2048
ITERS = 5
BR = 16

COEF_A = 3.4445
COEF_B = -4.775
COEF_C = 2.0315
DECAY = 0.95
EPSILON = 1e-07
ROW_SCALE = 0.2

F32 = jnp.float32
BF16 = jnp.bfloat16
CORES = 2
LANES = 128
GROUP = 8
HALF = GROUP // 2
SIZE = BR * GROUP
REST = 3
SENT = 2 * (GROUP + REST)


def dot(a, b):
    return jnp.dot(a, b, preferred_element_type=F32)


def split(a):
    high = a.astype(BF16)
    return high, (a - high.astype(F32)).astype(BF16)


def pack(rows):
    owners = BR
    count, width = rows.shape
    first = owners * GROUP
    halves = rows[:first].reshape(owners, GROUP, 2, LANES).swapaxes(1, 2).reshape(owners, 2 * GROUP, LANES)
    others = jnp.pad(rows[first:], ((0, first + owners * REST - count), (0, 0)))
    others = others.reshape(owners, REST, 2, LANES).swapaxes(1, 2).reshape(owners, 2 * REST, LANES)
    return jnp.concatenate([halves, others], axis=1).reshape(owners, -1, 2, LANES)


def unpack(pairs, count):
    owners = BR
    first = owners * GROUP
    tiles = pairs.reshape(owners, -1, LANES)
    halves = tiles[:, : 2 * GROUP].reshape(owners, 2, GROUP, LANES).swapaxes(1, 2).reshape(first, 2 * LANES)
    others = tiles[:, 2 * GROUP :].reshape(owners, 2, REST, LANES).swapaxes(1, 2).reshape(-1, 2 * LANES)
    return jnp.concatenate([halves, others[: count - first]], axis=0)


def row_groups(rows_ref):
    wide = rows_ref[...].astype(F32)
    empty = jnp.zeros((HALF - REST, LANES), F32)
    tiles = [[], [], []]
    for row in range(BR):
        base = row * SENT
        tiles[0].append(wide[base : base + GROUP])
        tiles[1].append(wide[base + GROUP : base + 2 * GROUP])
        base += 2 * GROUP
        tiles[2] += [wide[base : base + REST], empty, wide[base + REST : base + 2 * REST], empty]
    tiles = [jnp.concatenate(tile, axis=0) for tile in tiles]
    return [jnp.concatenate(tiles[:2], axis=1), tiles[2]]


def same_slot():
    rows = lax.broadcasted_iota(jnp.int32, (SIZE, SIZE), 0)
    columns = lax.broadcasted_iota(jnp.int32, (SIZE, SIZE), 1)
    return rows % GROUP == columns % GROUP


def gram_kernel(rows_ref, gram_ref):
    mask = same_slot()
    parts = []
    for rows in row_groups(rows_ref):
        rows = rows.astype(BF16)
        full = lax.dot_general(rows, rows, (((1,), (1,)), ((), ())), preferred_element_type=F32)
        parts.append(jnp.sum(jnp.where(mask, full, 0.0).reshape(BR, GROUP, SIZE), axis=1))
    halves = parts[1]
    low_half = lax.broadcasted_iota(jnp.int32, halves.shape, 1) % GROUP < HALF
    halves = halves + jnp.where(low_half, pltpu.roll(halves, SIZE - HALF, 1), pltpu.roll(halves, HALF, 1))
    parts[1] = jnp.where(low_half[:GROUP], halves[:GROUP], halves[GROUP:])
    packed = jnp.concatenate(parts, axis=0)
    for peer in range(gram_ref.shape[0]):
        gram_ref[peer] = packed


def unfold(total, group):
    if group == 0:
        return total[:BR]
    folded = total[BR:]
    low_half = lax.broadcasted_iota(jnp.int32, folded.shape, 1) % GROUP < HALF
    upper = jnp.where(low_half, folded, pltpu.roll(folded, HALF, 1))
    lower = jnp.where(low_half, pltpu.roll(folded, SIZE - HALF, 1), folded)
    return jnp.concatenate([upper, lower], axis=0)


def sweep_kernel(grams_ref, rows_ref, momentum_ref, out_ref, momentum_out_ref, done):
    written = pltpu.make_async_copy(momentum_ref, momentum_out_ref, done)
    written.start()
    mask = same_slot()
    same = lax.broadcasted_iota(jnp.int32, (SIZE, SIZE), 0) == lax.broadcasted_iota(jnp.int32, (SIZE, SIZE), 1)
    total = jnp.sum(grams_ref[...], axis=0)
    grams = []
    currents = []
    for group, rows in enumerate(row_groups(rows_ref)):
        gram = unfold(total, group)
        full = jnp.broadcast_to(gram[:, None, :], (BR, GROUP, SIZE)).reshape(SIZE, SIZE)
        full = jnp.where(mask, full, 0.0)
        by_column = jnp.sum(jnp.where(same, full, 0.0), axis=0, keepdims=True)
        squares = jnp.sum(jnp.where(mask, by_column, 0.0), axis=1, keepdims=True)
        norm = jnp.sqrt(squares) + EPSILON
        inverse = 1.0 / norm
        grams.append(full * (inverse * inverse))
        currents.append((rows / norm).astype(BF16))
    for sweep_index in range(ITERS):
        parts = [split(gram) for gram in grams]
        squared = [dot(part[0], part[0]) for part in parts]
        polynomials = [
            (COEF_B * part[0].astype(F32) + COEF_C * square).astype(BF16) for part, square in zip(parts, squared)
        ]
        if sweep_index + 1 < ITERS:
            lefts = [
                COEF_A * gram + dot(jnp.concatenate([poly, poly], axis=1), jnp.concatenate(part, axis=0))
                for gram, poly, part in zip(grams, polynomials, parts)
            ]
        currents = [
            (COEF_A * current.astype(F32) + dot(poly, current)).astype(BF16)
            for current, poly in zip(currents, polynomials)
        ]
        if sweep_index + 1 < ITERS:
            parts = [split(left) for left in lefts]
            grams = [
                COEF_A * left + dot(jnp.concatenate(part, axis=1), jnp.concatenate([poly, poly], axis=0))
                for left, poly, part in zip(lefts, polynomials, parts)
            ]
    factor = ROW_SCALE * (float(R) ** 0.5)
    first, second = [(current.astype(F32) * factor) for current in currents]
    pieces = []
    for row in range(BR):
        base = row * GROUP
        pieces += [first[base : base + GROUP, :LANES], first[base : base + GROUP, LANES:]]
        pieces += [second[base : base + REST], second[base + HALF : base + HALF + REST]]
    out_ref[...] = jnp.concatenate(pieces, axis=0).astype(BF16)
    written.wait()


def vmem_call(kernel, shape, dtype, count, flops):
    return pl.pallas_call(
        kernel,
        out_shape=jax.ShapeDtypeStruct(shape, dtype),
        in_specs=[pl.BlockSpec(memory_space=pltpu.VMEM)] * count,
        out_specs=pl.BlockSpec(memory_space=pltpu.VMEM),
        compiler_params=pltpu.CompilerParams(vmem_limit_bytes=4 << 20),
        cost_estimate=pl.CostEstimate(flops=flops, bytes_accessed=0, transcendentals=0),
    )


def owner_groups():
    chunks = C // 256
    return [[(row * 5 + 9) % BR * chunks + chunk for row in range(BR)] for chunk in range(chunks)]


def chunk_groups():
    chunks = C // 256
    return [[row * chunks + (chunk ^ 2) for chunk in range(chunks)] for row in range(BR)]


def gather_sum(gradients):
    groups = lax.axis_size("dp")
    mats, blocks, width = gradients.shape
    core = lax.axis_index("dp") % CORES
    parts = gradients.reshape(mats, groups // CORES, CORES, blocks // groups, width)
    sent = lax.dynamic_index_in_dim(parts, 1 - core, 2, keepdims=False).astype(BF16)
    arrived = lax.ppermute(sent, "dp", [(i, i ^ 1) for i in range(groups)])
    _, again = lax.optimization_barrier((sent, gradients))
    again = again.reshape(parts.shape)
    own = lax.optimization_barrier(lax.dynamic_index_in_dim(again, core, 2, keepdims=False).astype(BF16))
    pair = (own.astype(F32) + arrived.astype(F32)).astype(BF16)
    order = (2, 1, 0, 3)
    pair = jnp.stack([pair[:, chip] for chip in order])
    chips = [[chip * CORES + side for chip in order] for side in range(CORES)]
    arrived = lax.all_to_all(pair, "dp", 0, 0, tiled=True, axis_index_groups=chips)
    return jnp.sum(arrived.astype(F32), axis=0)


def shards(gradients, momentum):
    mats, local, width = momentum.shape
    count = mats * local
    summed = gather_sum(gradients[0])
    momentum_next = DECAY * momentum + summed
    nesterov = (summed + DECAY * momentum_next).astype(BF16).reshape(count, width)
    outgoing = pack(nesterov)
    rows = lax.all_to_all(outgoing, "shard", 0, 0, tiled=True, axis_index_groups=owner_groups())
    rows = rows.reshape(BR * SENT, LANES)
    chunks = C // width
    parts = vmem_call(gram_kernel, (chunks, BR + GROUP, SIZE), F32, 1, 0)(rows)
    grams = lax.all_to_all(parts, "shard", 0, 0, tiled=True, axis_index_groups=chunk_groups())
    finished, momentum_out = pl.pallas_call(
        sweep_kernel,
        out_shape=[
            jax.ShapeDtypeStruct(rows.shape, BF16),
            jax.ShapeDtypeStruct(momentum.shape, F32),
        ],
        in_specs=[pl.BlockSpec(memory_space=pltpu.VMEM)] * 3,
        out_specs=[pl.BlockSpec(memory_space=pltpu.VMEM), pl.BlockSpec(memory_space=pl.ANY)],
        scratch_shapes=[pltpu.SemaphoreType.DMA],
        compiler_params=pltpu.CompilerParams(vmem_limit_bytes=4 << 20),
    )(grams, rows, momentum_next)
    finished = finished.reshape(outgoing.shape)
    returned = lax.all_to_all(finished, "shard", 0, 0, tiled=True, axis_index_groups=owner_groups())
    return momentum_out, unpack(returned, count).reshape(momentum.shape)


def solution(mesh):
    placed = (P("dp", None, None, "shard"), P(None, "dp", "shard"))
    return jax.shard_map(
        shards,
        mesh=mesh,
        in_specs=placed,
        out_specs=(P(None, "dp", "shard"), P(None, "dp", "shard")),
        check_vma=False,
    )
```
